128 devices in a mesh: tm: 8 (over y, core), rows: 16 (over x, z).
Axes of the slice: x: 4, y: 4, z: 4, core: 2. Of those that a mesh axis runs over, the one named last changes fastest.
Arguments:
- latents: bfloat16 [16, 64, 128, 384], P('tm', 'rows'), may hold values from -6 to 6
- reward_weight: bfloat16 [16, 64, 128, 384], P('tm', 'rows'), may hold values from -6 to 6
- norm_gain: float32 [384], replicated, may hold values from 0.1 to 1.9
- conv_weight: bfloat16 [27, 384, 384], replicated, may hold values from -0.0625 to 0.0625
- scored_frames: int32 [8], replicated, may hold values from 0 to 15, as said below
Outputs:
- grad_latents: bfloat16 [16, 64, 128, 384], P('tm', 'rows')
- grad_weight: float32 [10368, 384], P(('tm', 'rows'))
- grad_gain: float32 [384], replicated
The draws below stay inside these ranges and needn't reach their ends.
Inputs may be any that keep to these rules, and one draw needn't show every extreme that they name: `scored_frames`: distinct latent frame indices; the first frame 0 and the last frame 16 - 1 are always scored.
All inputs are finite; a program needn't handle non-finite values.
Results may differ from the reference program's by a relative error of at most 0.015.
Values may be sent and summed in bfloat16 or wider, within the bound.
A program may use at most 256 MiB of HBM per device.

```python
import jax
import jax.numpy as jnp
from jax import lax

C = 384
WID = 128
FRAMES = 16
HEIGHT = 64
SCORED = 8


def draw_scored_frames(key, part):
    order = (jax.random.permutation(key, FRAMES - 2) + 1).astype(jnp.int32)
    first = jnp.zeros((1,), jnp.int32)
    last = jnp.full((1,), FRAMES - 1, jnp.int32)
    return jnp.concatenate([first, order[:SCORED - 2], last], axis=0)


def levels(own_key, extent, shards, low, largest):
    factor_of = 1.0
    for axis_at, shards_of in shards:
        heights = jax.random.uniform(jax.random.fold_in(jax.random.fold_in(own_key, 6), axis_at), (shards_of,), jnp.float32, low / len(shards), largest / len(shards))
        factor_of = factor_of * jnp.repeat(jnp.exp(heights), extent[axis_at] // shards_of).reshape((-1,) + (1,) * (len(extent) - 1 - axis_at))
    return factor_of


def gaussian(own_key, shape, spread, limit, cuts=(), kind=jnp.bfloat16):
    entries = jax.random.normal(own_key, shape, jnp.float32) * spread
    if len(cuts) > 0:
        entries = levels(own_key, shape, cuts, -0.22, 0.18) * entries
    return jnp.clip(entries, min=-limit, max=limit).astype(kind)


def setup_inputs(seed: int = 0) -> dict:
    keys = jax.random.split(jax.random.key(seed), 6)
    latents = gaussian(keys[0], (FRAMES, HEIGHT, WID, C), 1.0, 6.0, ((0, 8), (1, 16)))
    reward_weight = gaussian(keys[1], (FRAMES, HEIGHT, WID, C), 1.0, 6.0, ((0, 8), (1, 16)))
    norm_gain = jnp.clip(1.0 + 0.18 * jax.random.normal(keys[2], (C,), jnp.float32), 0.1, 1.9)
    conv_weight = gaussian(keys[3], (27, C, C), (27 * C) ** -0.5, 0.0625)
    scored_frames = draw_scored_frames(jax.random.fold_in(keys[5], 71), 0)
    return {"latents": latents, "reward_weight": reward_weight, "norm_gain": norm_gain, "conv_weight": conv_weight, "scored_frames": scored_frames}


EPSILON = 1e-06

def slope(value):
    sigmoid_v = jax.nn.sigmoid(value)
    return sigmoid_v * (1.0 + value * (1.0 - sigmoid_v))

def tap_product(left, right):
    return jnp.dot(left.astype(jnp.float32), right.astype(jnp.float32), precision=lax.Precision.HIGHEST)

def reference(latents, reward_weight, norm_gain, conv_weight, scored_frames):
    frames, height, columns, channels = latents.shape
    cell_count = frames * height * columns
    wide = latents.astype(jnp.float32)
    inverse = lax.rsqrt(lax.optimization_barrier(jnp.mean(wide * wide, axis=-1, keepdims=True)) + EPSILON)
    normed = wide * inverse
    activated = normed * norm_gain
    soft = jax.nn.silu(activated).astype(jnp.bfloat16)
    soft_pad = jnp.pad(soft, ((2, 0), (1, 1), (1, 1), (0, 0)))
    output = wide
    for offset in range(27):
        frame_off, row_off, col_off = (offset // 9, offset // 3 % 3, offset % 3)
        window = soft_pad[frame_off:frame_off + frames, row_off:row_off + height, col_off:col_off + columns].reshape(cell_count, channels)
        output = output + tap_product(window, conv_weight[offset]).reshape(wide.shape)
    scored_mask = jnp.any(jnp.arange(frames, dtype=jnp.int32)[:, None] == scored_frames[None, :], axis=1).astype(jnp.float32)
    grad_out = (scored_mask[:, None, None, None] * reward_weight.astype(jnp.float32) * slope(output)).astype(jnp.bfloat16)
    grad_flat = grad_out.reshape(cell_count, channels)
    grad_pad = jnp.pad(grad_out, ((0, 2), (1, 1), (1, 1), (0, 0)))
    grad_soft = jnp.zeros(wide.shape, jnp.float32)
    blocks = []
    for offset in range(27):
        frame_off, row_off, col_off = (offset // 9, offset // 3 % 3, offset % 3)
        window = grad_pad[2 - frame_off:2 - frame_off + frames, 2 - row_off:2 - row_off + height, 2 - col_off:2 - col_off + columns].reshape(cell_count, channels)
        grad_soft = grad_soft + tap_product(window, conv_weight[offset].T).reshape(wide.shape)
        source = soft_pad[frame_off:frame_off + frames, row_off:row_off + height, col_off:col_off + columns].reshape(cell_count, channels)
        blocks.append(tap_product(source.T, grad_flat))
    grad_weight = jnp.concatenate(blocks, axis=0)
    grad_act = grad_soft * slope(activated)
    grad_gain = lax.optimization_barrier(jnp.sum(grad_act * normed, axis=(0, 1, 2)))
    scaled = grad_act * norm_gain
    grad_latents = (grad_out.astype(jnp.float32) + inverse * (scaled - normed * lax.optimization_barrier(jnp.mean(scaled * normed, axis=-1, keepdims=True)))).astype(jnp.bfloat16)
    return (grad_latents, grad_weight, grad_gain)
```

```python
import functools

import jax
import jax.numpy as jnp
from jax import lax
from jax.experimental import pallas as pl
from jax.experimental.pallas import tpu as pltpu
from jax.sharding import PartitionSpec as P

MESH = pl.DeviceIdType.MESH
EPSILON = 1e-06
BF = jnp.bfloat16
F32 = jnp.float32
FR, HT, WD, CH = 2, 4, 128, 384
FLAT = HT * WD
OWN = 81
PAD = 96
TAPROWS = 27 * CH
ORDERS = ((0, 1, 2), (1, 2, 0), (2, 0, 1))


def sigmoid(value):
    return 0.5 + 0.5 * jnp.tanh(0.5 * value)


def slope(value):
    s = sigmoid(value)
    return s * (1.0 + value * (1.0 - s))


def normalise(cells):
    wide = cells.astype(F32)
    inverse = lax.rsqrt(jnp.mean(wide * wide, axis=-1, keepdims=True) + EPSILON)
    return wide, inverse, wide * inverse


def down(x):
    row = lax.broadcasted_iota(jnp.int32, x.shape, 0)
    return jnp.where(row == 0, 0.0, pltpu.roll(x, 1, 0))


def up(x):
    row = lax.broadcasted_iota(jnp.int32, x.shape, 0)
    return jnp.where(row == x.shape[0] - 1, 0.0, pltpu.roll(x, x.shape[0] - 1, 0))


def kernel(
    lat, rew, gain, wgt_hbm, scored,
    out_lat, out_w, out_gain,
    wgt, ext, extt, gout, gsh, prod, gw,
    cs, cr, r1, r2, r3, r4,
    gacc, gt, gx, gz, gmid,
    wsem, hs, hr, ks, kr, css, crs, ss, rs, gss, grs,
):
    tm = lax.axis_index("tm")
    row = lax.axis_index("rows")
    core = tm % 2
    place = (tm // 2, row // 4, row % 4)

    def device(coords, c):
        return {"tm": coords[0] * 2 + c, "rows": coords[1] * 4 + coords[2]}

    def flip(v):
        return v + 1 - 2 * (v % 2)

    other = []
    for v in place:
        second = core * flip(v) + (1 - core) * (3 - v)
        first = core * (3 - v) + (1 - core) * flip(v)
        other.append((v, second, first, (v + 2) % 4))

    def peer(axis, q):
        coords = list(place)
        coords[axis] = other[axis][q]
        return device(coords, core)

    def pick(axis, q):
        if isinstance(q, int):
            return other[axis][q]
        o = other[axis]
        return jnp.where(q == 0, o[0], jnp.where(q == 1, o[1], jnp.where(q == 2, o[2], o[3])))

    tm_next, tm_prev = (tm + 1) % 8, (tm + 7) % 8
    row_next, row_prev = (row + 1) % 16, (row + 15) % 16
    twin = {"tm": tm + 1 - 2 * core, "rows": row}

    barrier = pltpu.get_barrier_semaphore()
    greeted = 0
    for dt, dr in ((1, 0), (7, 0), (0, 1), (0, 15), (1, 1), (1, 15), (7, 1), (7, 15)):
        pl.semaphore_signal(
            barrier, 1, device_id={"tm": (tm + dt) % 8, "rows": (row + dr) % 16}, device_id_type=MESH
        )
        greeted += 1
    for dt in range(2, 7):
        pl.semaphore_signal(barrier, 1, device_id={"tm": (tm + dt) % 8, "rows": row}, device_id_type=MESH)
        greeted += 1
    for axis in (1, 2):
        for q in (1, 2, 3):
            pl.semaphore_signal(barrier, 1, device_id=peer(axis, q), device_id_type=MESH)
            greeted += 1

    load = pltpu.make_async_copy(wgt_hbm, wgt, wsem)
    load.start()

    g_row = gain[...]

    def soften(cells, keep=None):
        _, _, normed = normalise(cells)
        act = normed * g_row
        value = act * sigmoid(act)
        if keep is not None:
            value = value * keep
        return value.astype(BF)

    def own_soft(i, _):
        f, r = i // HT, i % HT
        ext[2 + f, 1 + r] = soften(lat[f, r])
        return 0

    lax.fori_loop(0, FR * HT, own_soft, 0)

    pl.semaphore_wait(barrier, greeted)

    def send(src, dst, a, b, target):
        copy = pltpu.make_async_remote_copy(
            src_ref=src, dst_ref=dst, send_sem=a, recv_sem=b, device_id=target, device_id_type=MESH
        )
        copy.start()
        return copy

    def halo(copies, sems, src, dst, i, dt, dr):
        copies.append(
            send(src, dst, sems[0].at[i], sems[1].at[i], {"tm": (tm + dt) % 8, "rows": (row + dr) % 16})
        )

    copies = []
    pair = pl.ds(0, 2)
    halo(copies, (hs, hr), lat, ext.at[pair, pl.ds(1, HT)], 0, 1, 0)
    halo(copies, (hs, hr), lat.at[pair, HT - 1], ext.at[pl.ds(2, 2), 0], 1, 0, 1)
    halo(copies, (hs, hr), lat.at[pair, 0], ext.at[pl.ds(2, 2), HT + 1], 2, 0, 15)
    halo(copies, (hs, hr), lat.at[pair, HT - 1], ext.at[pair, 0], 3, 1, 1)
    halo(copies, (hs, hr), lat.at[pair, 0], ext.at[pair, HT + 1], 4, 1, 15)
    for copy in copies:
        copy.wait_recv()

    has_prev = jnp.where(tm > 0, 1.0, 0.0).astype(F32)
    has_top = jnp.where(row > 0, 1.0, 0.0).astype(F32)
    has_bot = jnp.where(row < 15, 1.0, 0.0).astype(F32)

    def halo_mid(i, _):
        f, r = i // HT, 1 + i % HT
        ext[f, r] = soften(ext[f, r], has_prev)
        return 0

    lax.fori_loop(0, FR * HT, halo_mid, 0)

    def halo_edge(f, _):
        keep = jnp.where(f < 2, has_prev, 1.0)
        ext[f, 0] = soften(ext[f, 0], keep * has_top)
        ext[f, HT + 1] = soften(ext[f, HT + 1], keep * has_bot)
        return 0

    lax.fori_loop(0, 4, halo_edge, 0)

    load.wait()

    def forward(f, _):
        left = jnp.concatenate(
            [ext[f + t // 3, pl.ds(t % 3, HT)].reshape(FLAT, CH) for t in range(9)], axis=1
        )
        right = jnp.concatenate(
            [jnp.concatenate([wgt[3 * t + c] for c in range(3)], axis=1) for t in range(9)], axis=0
        )
        prod[...] = jnp.dot(left, right, preferred_element_type=F32)
        frame = tm * FR + f
        mask = jnp.float32(0.0)
        for i in range(8):
            mask = jnp.maximum(mask, jnp.where(scored[i] == frame, 1.0, 0.0))

        def one_row(r, _):
            at = pl.ds(pl.multiple_of(r * WD, WD), WD)
            conv = down(prod[at, 0:CH]) + prod[at, CH : 2 * CH] + up(prod[at, 2 * CH : 3 * CH])
            value = lat[f, r].astype(F32) + conv
            grad = mask * rew[f, r].astype(F32) * slope(value)
            low = grad.astype(BF)
            wide = low.astype(F32)
            gout[f, 1 + r] = low
            to = pl.ds(pl.multiple_of(f * FLAT + r * WD, WD), WD)
            gsh[to, 0:CH] = up(wide).astype(BF)
            gsh[to, CH : 2 * CH] = low
            gsh[to, 2 * CH : 3 * CH] = down(wide).astype(BF)
            return 0

        lax.fori_loop(0, HT, one_row, 0)
        return 0

    lax.fori_loop(0, FR, forward, 0)

    gcopies = []
    halo(gcopies, (ks, kr), gout.at[pair, pl.ds(1, HT)], gout.at[pl.ds(2, 2), pl.ds(1, HT)], 0, 7, 0)
    halo(gcopies, (ks, kr), gout.at[pair, HT], gout.at[pair, 0], 1, 0, 1)
    halo(gcopies, (ks, kr), gout.at[pair, 1], gout.at[pair, HT + 1], 2, 0, 15)
    halo(gcopies, (ks, kr), gout.at[pair, HT], gout.at[pl.ds(2, 2), 0], 3, 7, 1)
    halo(gcopies, (ks, kr), gout.at[pair, 1], gout.at[pl.ds(2, 2), HT + 1], 4, 7, 15)

    def turn(f, _):
        for half in range(2):
            cells = ext[f, pl.ds(3 * half, 3)].reshape(3 * WD, CH)
            extt[:, pl.ds(pl.multiple_of(f * 6 * WD + half * 3 * WD, WD), 3 * WD)] = cells.T
        return 0

    lax.fori_loop(0, 4, turn, 0)
    gw[:, TAPROWS:, :] = jnp.zeros((3, 16, 128), F32)

    core_copies = []

    def core_send(k):
        def one(r, _):
            at = ((2 * k + 1 - core) * 16 + r) * OWN
            for p in range(3):
                cs[(k * 16 + r) * 3 + p] = gw[p, pl.ds(at, PAD)].astype(BF)
            return 0

        lax.fori_loop(0, 16, one, 0)
        core_copies.append(send(cs.at[pl.ds(48 * k, 48)], cr.at[pl.ds(48 * k, 48)], css.at[k], crs.at[k], twin))

    for a in range(3):
        left = jnp.concatenate(
            [
                jnp.concatenate(
                    [extt[:, ((f + a) * 6 + b) * WD : ((f + a) * 6 + b) * WD + FLAT] for f in range(FR)], axis=1
                )
                for b in range(3)
            ],
            axis=0,
        )
        part = jnp.dot(left, gsh[...], preferred_element_type=F32)
        for b in range(3):
            for c in range(3):
                at = (9 * a + 3 * b + c) * CH
                for p in range(3):
                    lane = c * CH + p * 128
                    gw[p, at : at + CH, :] = part[b * CH : b * CH + CH, lane : lane + 128]
        for k in ((0,), (1,), (2, 3))[a]:
            core_send(k)

    def total(p, q):
        coords = [None, None, None]
        for axis, at in zip(ORDERS[p], q):
            coords[axis] = pick(axis, at)
        lane = coords[1] * 4 + coords[2]
        start = ((2 * coords[0] + core) * 16 + lane) * OWN
        return gw[p, pl.ds(start, PAD)] + cr[(coords[0] * 16 + lane) * 3 + p].astype(F32)

    for copy in core_copies:
        copy.wait()

    def step1(i, _):
        for p in range(3):
            cs[32 * p + i] = total(p, (2 + i // 16, (i // 4) % 4, i % 4)).astype(BF)
        return 0

    lax.fori_loop(0, 32, step1, 0)
    step1_copies = [
        send(cs.at[pl.ds(32 * p, 32)], r1.at[p], ss.at[p], rs.at[p], peer(ORDERS[p][0], 2)) for p in range(3)
    ]

    for copy in gcopies:
        copy.wait()

    @pl.when(tm == 7)
    def _():
        gout[2:4] = jnp.zeros((2, HT + 2, WD, CH), BF)

    @pl.when(row == 0)
    def _():
        gout[:, 0] = jnp.zeros((4, WD, CH), BF)

    @pl.when(row == 15)
    def _():
        gout[:, HT + 1] = jnp.zeros((4, WD, CH), BF)

    gacc[...] = jnp.zeros_like(gacc)

    def backward(f):
        left = jnp.concatenate(
            [gout[f + 2 - t // 3, pl.ds(2 - t % 3, HT)].reshape(FLAT, CH) for t in range(9)], axis=1
        )
        right = jnp.concatenate([wgt[3 * t : 3 * t + 3].reshape(3 * CH, CH) for t in range(9)], axis=1)
        prod[...] = lax.dot_general(left, right, (((1,), (1,)), ((), ())), preferred_element_type=F32)

        def one_row(r, _):
            at = pl.ds(pl.multiple_of(r * WD, WD), WD)
            grad_soft = up(prod[at, 0:CH]) + prod[at, CH : 2 * CH] + down(prod[at, 2 * CH : 3 * CH])
            _, inverse, normed = normalise(lat[f, r])
            grad_act = grad_soft * slope(normed * g_row)
            per_cell = grad_act * normed
            gacc[...] += jnp.sum(per_cell.reshape(WD // 8, 8, CH), axis=0)
            scaled = grad_act * g_row
            mean = jnp.mean(per_cell * g_row, axis=-1, keepdims=True)
            out_lat[f, r] = (gout[f, 1 + r].astype(F32) + inverse * (scaled - normed * mean)).astype(BF)
            return 0

        lax.fori_loop(0, HT, one_row, 0)

    backward(0)

    for copy in step1_copies:
        copy.wait_recv()

    def step2(i, _):
        for p in range(3):
            value = total(p, (1, i // 4, i % 4)) + r1[p, 16 + i].astype(F32)
            cs[96 + 16 * p + i] = value.astype(BF)
        return 0

    lax.fori_loop(0, 16, step2, 0)
    step2_copies = [
        send(cs.at[pl.ds(96 + 16 * p, 16)], r2.at[p], ss.at[3 + p], rs.at[3 + p], peer(ORDERS[p][0], 1)) for p in range(3)
    ]

    backward(1)

    gain_copies = []
    gt[tm] = gacc[...]
    for d in range(1, 8):
        gain_copies.append(
            send(gacc, gt.at[tm], gss.at[d - 1], grs.at[d - 1], {"tm": (tm + d) % 8, "rows": row})
        )

    for copy in step2_copies:
        copy.wait_recv()

    def step3(i, _):
        q2, q3 = 1 + i // 4, i % 4
        at = q2 * 4 + q3
        for p in range(3):
            value = total(p, (0, q2, q3)) + r1[p, at].astype(F32) + r2[p, at].astype(F32)
            cs[144 + 12 * p + i] = value.astype(BF)
        return 0

    lax.fori_loop(0, 12, step3, 0)
    step3_copies = []
    for p in range(3):
        for q in (1, 2, 3):
            n = 6 + 3 * p + q - 1
            part = pl.ds(4 * (q - 1), 4)
            step3_copies.append(
                send(cs.at[pl.ds(144 + 12 * p + 4 * (q - 1), 4)], r3.at[p, part], ss.at[n], rs.at[n], peer(ORDERS[p][1], q))
            )

    for copy in gain_copies:
        copy.wait()
    gsum = gt[0]
    for d in range(1, 8):
        gsum = gsum + gt[d]
    gmid[0] = gsum
    gx[place[1]] = gsum
    xcopies = [
        send(gmid.at[0], gx.at[place[1]], gss.at[6 + q], grs.at[6 + q], peer(1, q)) for q in (1, 2, 3)
    ]

    for copy in step3_copies:
        copy.wait_recv()

    def step4(i, _):
        q3 = 1 + i
        for p in range(3):
            value = total(p, (0, 0, q3)) + r1[p, q3].astype(F32) + r2[p, q3].astype(F32)
            for q in range(3):
                value = value + r3[p, 4 * q + q3].astype(F32)
            cs[180 + 3 * p + i] = value.astype(BF)
        return 0

    lax.fori_loop(0, 3, step4, 0)
    step4_copies = []
    for p in range(3):
        for q in (1, 2, 3):
            n = 15 + 3 * p + q - 1
            step4_copies.append(
                send(cs.at[180 + 3 * p + q - 1], r4.at[p, q - 1], ss.at[n], rs.at[n], peer(ORDERS[p][2], q))
            )

    for copy in xcopies:
        copy.wait()
    gsum = gx[0] + gx[1] + gx[2] + gx[3]
    gmid[1] = gsum
    gz[place[2]] = gsum
    zcopies = [
        send(gmid.at[1], gz.at[place[2]], gss.at[9 + q], grs.at[9 + q], peer(2, q)) for q in (1, 2, 3)
    ]

    for copy in step4_copies:
        copy.wait_recv()
    for p in range(3):
        value = total(p, (0, 0, 0)) + r1[p, 0].astype(F32) + r2[p, 0].astype(F32)
        for q in range(3):
            value = value + r3[p, 4 * q].astype(F32)
        for q in range(3):
            value = value + r4[p, q].astype(F32)
        out_w[:, p * 128 : p * 128 + 128] = value[:OWN]

    for copy in zcopies:
        copy.wait()
    gsum = gz[0] + gz[1] + gz[2] + gz[3]
    out_gain[...] = jnp.sum(gsum, axis=0, keepdims=True)

    for copy in copies + step1_copies + step2_copies + step3_copies + step4_copies:
        copy.wait_send()


def shards(latents, reward_weight, norm_gain, conv_weight, scored_frames):
    vm = pl.BlockSpec(memory_space=pltpu.VMEM)
    dma = pltpu.SemaphoreType.DMA
    blocks = lambda *lead: pltpu.VMEM(lead + (PAD, 128), BF)
    lat, wsum, gsum = pl.pallas_call(
        kernel,
        out_shape=(
            jax.ShapeDtypeStruct((FR, HT, WD, CH), BF),
            jax.ShapeDtypeStruct((OWN, CH), F32),
            jax.ShapeDtypeStruct((1, CH), F32),
        ),
        in_specs=[vm, vm, vm, pl.BlockSpec(memory_space=pl.ANY), pl.BlockSpec(memory_space=pltpu.SMEM)],
        out_specs=(vm, vm, vm),
        scratch_shapes=[
            pltpu.VMEM((27, CH, CH), BF),
            pltpu.VMEM((4, HT + 2, WD, CH), BF),
            pltpu.VMEM((CH, 4 * (HT + 2) * WD), BF),
            pltpu.VMEM((4, HT + 2, WD, CH), BF),
            pltpu.VMEM((FR * FLAT, 3 * CH), BF),
            pltpu.VMEM((FLAT, 3 * CH), F32),
            pltpu.VMEM((3, TAPROWS + 16, 128), F32),
            blocks(192),
            blocks(192),
            blocks(3, 32),
            blocks(3, 16),
            blocks(3, 12),
            blocks(3, 3),
            pltpu.VMEM((8, CH), F32),
            pltpu.VMEM((8, 8, CH), F32),
            pltpu.VMEM((4, 8, CH), F32),
            pltpu.VMEM((4, 8, CH), F32),
            pltpu.VMEM((2, 8, CH), F32),
            dma,
            dma((5,)),
            dma((5,)),
            dma((5,)),
            dma((5,)),
            dma((4,)),
            dma((4,)),
            dma((24,)),
            dma((24,)),
            dma((13,)),
            dma((13,)),
        ],
        compiler_params=pltpu.CompilerParams(
            collective_id=0, has_side_effects=True, vmem_limit_bytes=61 * 1024 * 1024
        ),
        cost_estimate=pl.CostEstimate(flops=24_500_000_000, bytes_accessed=12_000_000, transcendentals=1_500_000),
    )(latents, reward_weight, norm_gain.reshape(1, CH), conv_weight, scored_frames)
    return lat, wsum, gsum.reshape(CH)


def solution(mesh):
    placed = (P("tm", "rows", None, None), P("tm", "rows", None, None), P(), P(), P())
    return jax.shard_map(
        shards,
        mesh=mesh,
        in_specs=placed,
        out_specs=(P("tm", "rows", None, None), P(("tm", "rows"), None), P()),
        check_vma=False,
    )
```

```python
import functools

import jax
import jax.numpy as jnp
from jax import lax
from jax.experimental import pallas as pl
from jax.experimental.pallas import tpu as pltpu
from jax.sharding import PartitionSpec as P

MESH = pl.DeviceIdType.MESH
EPSILON = 1e-06
BF = jnp.bfloat16
F32 = jnp.float32
FR, HT, WD, CH = 2, 4, 128, 384
FLAT = HT * WD
OWN = 81
PAD = 96
SUB = 32
SLAB = 16 * OWN
TAPROWS = 27 * CH
ORDERS = ((0, 1, 2), (1, 2, 0), (2, 0, 1))
CHUNKS = ((0, 1), (2,))


def sigmoid(value):
    return 0.5 + 0.5 * jnp.tanh(0.5 * value)


def slope(value):
    s = sigmoid(value)
    return s * (1.0 + value * (1.0 - s))


def normalise(cells):
    wide = cells.astype(F32)
    inverse = lax.rsqrt(jnp.mean(wide * wide, axis=-1, keepdims=True) + EPSILON)
    return wide, inverse, wide * inverse


def down(x):
    row = lax.broadcasted_iota(jnp.int32, x.shape, 0)
    return jnp.where(row == 0, 0.0, pltpu.roll(x, 1, 0))


def up(x):
    row = lax.broadcasted_iota(jnp.int32, x.shape, 0)
    return jnp.where(row == x.shape[0] - 1, 0.0, pltpu.roll(x, x.shape[0] - 1, 0))


def kernel(
    lat_hbm, rew_hbm, gain, wgt_hbm, scored,
    out_lat, out_w, out_gain,
    lat, rew, res, wgt, ext, extt, gout, gsh, prod, gw,
    cs, cr, r1, r2, r3, r4, fin,
    gacc, gt, gx, gz, gmid,
    wsem, osem, hs, hr, ks, kr, css, crs, ss, rs, gss, grs,
):
    tm = lax.axis_index("tm")
    row = lax.axis_index("rows")
    core = tm % 2
    place = (tm // 2, row // 4, row % 4)

    def device(coords, c):
        return {"tm": coords[0] * 2 + c, "rows": coords[1] * 4 + coords[2]}

    def flip(v):
        return v + 1 - 2 * (v % 2)

    other = []
    for v in place:
        second = core * flip(v) + (1 - core) * (3 - v)
        first = core * (3 - v) + (1 - core) * flip(v)
        other.append((v, second, first, (v + 2) % 4))

    def peer(axis, q):
        coords = list(place)
        coords[axis] = other[axis][q]
        return device(coords, core)

    def pick(axis, q):
        if isinstance(q, int):
            return other[axis][q]
        o = other[axis]
        return jnp.where(q == 0, o[0], jnp.where(q == 1, o[1], jnp.where(q == 2, o[2], o[3])))

    row_next, row_prev = (row + 1) % 16, (row + 15) % 16
    twin = {"tm": tm + 1 - 2 * core, "rows": row}

    barrier = pltpu.get_barrier_semaphore()
    partners = [{"tm": tm, "rows": row_next}, {"tm": tm, "rows": row_prev}]
    partners += [{"tm": (tm + d) % 8, "rows": row} for d in range(1, 8)]
    partners += [peer(axis, q) for axis in (1, 2) for q in (1, 2, 3)]
    for partner in partners:
        pl.semaphore_signal(barrier, 1, device_id=partner, device_id_type=MESH)

    load_lat = pltpu.make_async_copy(lat_hbm, lat, wsem.at[0])
    load = pltpu.make_async_copy(wgt_hbm, wgt, wsem.at[1])
    load_rew = pltpu.make_async_copy(rew_hbm, rew, wsem.at[2])
    load_lat.start()
    load.start()
    load_rew.start()

    g_row = gain[...].reshape(1, CH)
    zero_block = jnp.zeros((2, WD, CH), BF)

    def own_soft(i, _):
        f, r = i // HT, i % HT
        _, _, normed = normalise(lat[f, r])
        act = normed * g_row
        ext[2 + f, 1 + r] = (act * sigmoid(act)).astype(BF)
        return 0

    load_lat.wait()
    lax.fori_loop(0, FR * HT, own_soft, 0)

    def product(f, taps):
        left = jnp.concatenate(
            [ext[f + a, b : b + HT].reshape(FLAT, CH) for a, b in taps], axis=1
        )
        right = jnp.concatenate(
            [jnp.concatenate([wgt[9 * a + 3 * b + c] for c in range(3)], axis=1) for a, b in taps], axis=0
        )
        return jnp.dot(left, right, preferred_element_type=F32)

    load.wait()
    prod[0] = product(0, [(2, 1)])
    prod[1] = product(1, [(1, 1), (2, 1)])

    pl.semaphore_wait(barrier, len(partners))

    def copy_of(src, dst, a, b, target):
        return pltpu.make_async_remote_copy(
            src_ref=src, dst_ref=dst, send_sem=a, recv_sem=b, device_id=target, device_id_type=MESH
        )

    def send(*args):
        copy = copy_of(*args)
        copy.start()
        return copy

    class Halo:
        def __init__(self, ref, own, far, step, order, sems):
            self.own, self.far, self.ref, self.order = own, far, ref, order
            self.giver = core == (0 if step == 1 else 1)
            self.end = 0 if step == 1 else 7
            up_row, down_row = {"tm": tm, "rows": row_next}, {"tm": tm, "rows": row_prev}
            slab = {"tm": (tm + step) % 8, "rows": row}
            mine = pl.ds(own, 2)
            theirs = pl.ds(far, 2)

            def make(i, src, dst, target):
                return copy_of(src, dst, sems[0].at[i], sems[1].at[i], target)

            self.rows = [
                make(0, ref.at[mine, HT], ref.at[mine, 0], up_row),
                make(1, ref.at[mine, 1], ref.at[mine, HT + 1], down_row),
            ]
            self.edges, self.inner, self.relay = {}, {}, {}
            for k in order:
                self.edges[k] = [
                    make(2 + 2 * k, ref.at[own + k, HT], ref.at[far + k, HT], slab),
                    make(3 + 2 * k, ref.at[own + k, 1], ref.at[far + k, 1], slab),
                ]
                inside = pl.ds(2, HT - 2)
                self.inner[k] = [make(6 + k, ref.at[own + k, inside], ref.at[far + k, inside], slab)]
                self.relay[k] = [
                    make(10 + 2 * k, ref.at[far + k, HT], ref.at[far + k, 0], up_row),
                    make(11 + 2 * k, ref.at[far + k, 1], ref.at[far + k, HT + 1], down_row),
                ]
            self.forward = [
                make(8, ref.at[mine, 0], ref.at[theirs, 0], twin),
                make(9, ref.at[mine, HT + 1], ref.at[theirs, HT + 1], twin),
            ]

        def begin(self):
            for copy in self.rows:
                copy.start()
            for k in self.order:
                for copy in self.edges[k]:
                    copy.start()
            for k in self.order:
                for copy in self.inner[k]:
                    copy.start()

        def take_rows(self):
            for copy in self.rows:
                copy.wait_recv()
            self.clear(self.own, 2)

            @pl.when(self.giver)
            def _():
                for copy in self.forward:
                    copy.start()

        def take_edges(self, k):
            for copy in self.edges[k]:
                copy.wait_recv()

            @pl.when(self.giver)
            def _():
                for copy in self.relay[k]:
                    copy.start()

        def take_rest(self, k):
            for copy in self.inner[k]:
                copy.wait_recv()

            @pl.when(self.giver)
            def _():
                for copy in self.relay[k]:
                    copy.wait()

            if k == self.order[0]:

                @pl.when(jnp.logical_not(self.giver))
                def _():
                    for copy in self.forward:
                        copy.wait_recv()

            self.clear(self.far + k, 1)

            @pl.when(tm == self.end)
            def _():
                self.ref[self.far + k] = jnp.zeros((HT + 2, WD, CH), BF)

        def clear(self, frame, count):
            @pl.when(row == 0)
            def _():
                self.ref[frame : frame + count, 0] = zero_block[:count]

            @pl.when(row == 15)
            def _():
                self.ref[frame : frame + count, HT + 1] = zero_block[:count]

        def finish(self):
            @pl.when(self.giver)
            def _():
                for copy in self.forward:
                    copy.wait_send()

            for copy in self.rows:
                copy.wait_send()
            for k in self.order:
                for copy in self.edges[k] + self.inner[k]:
                    copy.wait_send()

    soft_halo = Halo(ext, 2, 0, 1, (1, 0), (hs, hr))
    soft_halo.begin()

    def turn(f, rows):
        for r in rows:
            extt[:, (f * 6 + r) * WD : (f * 6 + r + 1) * WD] = ext[f, r].T

    def emit(f):
        frame = tm * FR + f
        mask = jnp.float32(0.0)
        for i in range(8):
            mask = jnp.maximum(mask, jnp.where(scored[i] == frame, 1.0, 0.0))

        def one_row(r, _):
            at = pl.ds(pl.multiple_of(r * WD, WD), WD)
            conv = down(prod[f, at, 0:CH]) + prod[f, at, CH : 2 * CH] + up(prod[f, at, 2 * CH : 3 * CH])
            value = lat[f, r].astype(F32) + conv
            grad = mask * rew[f, r].astype(F32) * slope(value)
            low = grad.astype(BF)
            wide = low.astype(F32)
            gout[f, 1 + r] = low
            to = pl.ds(pl.multiple_of(f * FLAT + r * WD, WD), WD)
            for c, shifted in enumerate((up(wide).astype(BF), low, down(wide).astype(BF))):
                gsh[to, c * 256 : c * 256 + 256] = shifted[:, :256]
                gsh[to, 768 + c * 128 : 896 + c * 128] = shifted[:, 256:]
            return 0

        lax.fori_loop(0, HT, one_row, 0)

    for f in (2, 3):
        turn(f, (1, 2, 3, 4))
    soft_halo.take_rows()
    prod[0] += product(0, [(2, 0), (2, 2)])
    soft_halo.take_edges(1)
    prod[1] += product(1, [(1, 0), (1, 2), (2, 0), (2, 2)])
    load_rew.wait()
    for f in (2, 3):
        turn(f, (0, 5))
    soft_halo.take_edges(0)
    soft_halo.take_rest(1)
    prod[1] += product(1, [(0, 0), (0, 1), (0, 2)])
    emit(1)
    prod[0] += product(0, [(1, 0), (1, 1), (1, 2)])
    turn(1, range(6))
    soft_halo.take_rest(0)
    prod[0] += product(0, [(0, 0), (0, 1), (0, 2)])
    emit(0)

    grad_halo = Halo(gout, 0, 2, -1, (0, 1), (ks, kr))
    grad_halo.begin()

    turn(0, range(6))
    gw[:, TAPROWS:, :] = jnp.zeros((3, 16, 128), F32)

    def start_of(block):
        return pl.multiple_of(block * OWN // 16 * 16, 16)

    def unit(n, count=1):
        return pl.ds(pl.multiple_of(SUB * n, SUB), SUB * count)

    class Chunk:
        def __init__(self, n):
            self.parts = CHUNKS[n]
            self.width = len(self.parts)
            self.base = 3 * sum(len(c) for c in CHUNKS[:n])
            self.sem = 24 * n
            self.csem = 3 * n
            self.core_copies = []
            self.copies = {}

        def area(self, blocks):
            return self.base * blocks

        def core_send(self, n, low, high):
            lead = self.base * 64 * SUB
            for k in range(low, high):
                for pi, p in enumerate(self.parts):
                    at = lead + (k * self.width + pi) * SLAB

                    def one(i, _):
                        step = SLAB // 9
                        src = pl.multiple_of((2 * k + 1 - core) * SLAB + i * step, 16)
                        dst = pl.multiple_of(at + i * step, 16)
                        cs[pl.ds(dst, step)] = gw[p, pl.ds(src, step)].astype(BF)
                        return 0

                    lax.fori_loop(0, 9, one, 0)
            rows = self.width * (high - low) * SLAB
            src = pl.ds(lead + low * self.width * SLAB, rows)
            dst = pl.ds(self.base // 3 * 4 * SLAB + low * self.width * SLAB, rows)
            self.core_copies.append(
                send(cs.at[src], cr.at[dst], css.at[self.csem + n], crs.at[self.csem + n], twin)
            )

        def core_done(self):
            for copy in self.core_copies:
                copy.wait()

        def total(self, pi, j, q):
            coords = [None, None, None]
            for axis, at in zip(ORDERS[j], q):
                coords[axis] = pick(axis, at)
            lane = coords[1] * 4 + coords[2]
            start = start_of((2 * coords[0] + core) * 16 + lane)
            held = gw[self.parts[pi], pl.ds(pl.multiple_of(start + SUB * j, 16), SUB)]
            near = start - (2 * coords[0] + core) * SLAB + SUB * j
            at = (self.base // 3 * 4 + coords[0] * self.width + pi) * SLAB + near
            return held + cr[pl.ds(pl.multiple_of(at, 16), SUB)].astype(F32)

        def got(self, ref, blocks, j, i, pi):
            return ref[unit(self.area(blocks) + (j * blocks + i) * self.width + pi)].astype(F32)

        def value(self, step, pi, j, q):
            value = self.total(pi, j, q)
            if step >= 2:
                value = value + self.got(r1, 32, j, (q[0] * 4 + q[1]) * 4 + q[2], pi)
            if step >= 3:
                value = value + self.got(r2, 16, j, q[1] * 4 + q[2], pi)
            if step >= 4:
                for n in range(3):
                    value = value + self.got(r3, 12, j, 4 * n + q[2], pi)
            if step >= 5:
                for n in range(3):
                    value = value + self.got(r4, 3, j, n, pi)
            return value

        def step(self, step):
            if step > 1:
                for copy in self.copies[step - 1]:
                    copy.wait_recv()
            first = (None, 0, 96, 144, 180)[step]
            blocks = (None, 32, 16, 12, 3)[step]
            into = (None, r1, r2, r3, r4)[step]
            place_of = (
                None,
                lambda i: (2 + i // 16, i // 4 % 4, i % 4),
                lambda i: (1, i // 4, i % 4),
                lambda i: (0, 1 + i // 4, i % 4),
                lambda i: (0, 0, 1 + i),
            )[step]
            lead = self.area(64) + first * self.width

            def one(i, _):
                for j in range(3):
                    for pi in range(self.width):
                        value = self.value(step, pi, j, place_of(i)).astype(BF)
                        cs[unit(lead + (j * blocks + i) * self.width + pi)] = value
                return 0

            lax.fori_loop(0, blocks, one, 0)
            out = []
            for j in range(3):
                axis = ORDERS[j][(None, 0, 0, 1, 2)[step]]
                for n, q in enumerate(((2,), (1,), (1, 2, 3), (1, 2, 3))[step - 1]):
                    span = blocks // (1 if step < 3 else 3) * self.width
                    at = j * blocks * self.width + n * span
                    sem = self.sem + (None, j, 3 + j, 6 + 3 * j + n, 15 + 3 * j + n)[step]
                    out.append(
                        send(
                            cs.at[unit(lead + at, span)],
                            into.at[unit(self.area(blocks) + at, span)],
                            ss.at[sem],
                            rs.at[sem],
                            peer(axis, q),
                        )
                    )
            self.copies[step] = out

        def last(self):
            for copy in self.copies[4]:
                copy.wait_recv()
            for pi, p in enumerate(self.parts):
                for j in range(3):
                    fin[p, SUB * j : SUB * j + SUB] = self.value(5, pi, j, (0, 0, 0))
            offset = (tm * 16 + row) * OWN % 16
            for p in self.parts:
                out_w[:, p * 128 : p * 128 + 128] = fin[p, pl.ds(offset, OWN)]

        def finish(self):
            for copies in self.copies.values():
                for copy in copies:
                    copy.wait_send()

    def outer(n, a):
        parts = CHUNKS[n]
        wide = 128 * len(parts)
        left = jnp.concatenate(
            [
                jnp.concatenate(
                    [extt[:, ((f + a) * 6 + b) * WD : ((f + a) * 6 + b) * WD + FLAT] for f in range(FR)], axis=1
                )
                for b in range(3)
            ],
            axis=0,
        )
        lanes = slice(384 * parts[0], 384 * parts[0] + 3 * wide)
        part = jnp.dot(left, gsh[:, lanes], preferred_element_type=F32)
        for b in range(3):
            for c in range(3):
                at = (9 * a + 3 * b + c) * CH
                for pi, p in enumerate(parts):
                    lane = c * wide + pi * 128
                    gw[p, at : at + CH, :] = part[b * CH : b * CH + CH, lane : lane + 128]

    one, two = Chunk(0), Chunk(1)
    outer(0, 0)
    one.core_send(0, 0, 1)
    outer(0, 1)
    one.core_send(1, 1, 2)
    grad_halo.take_rows()
    outer(0, 2)
    one.core_send(2, 2, 4)
    grad_halo.take_edges(0)
    outer(1, 0)
    grad_halo.take_edges(1)
    outer(1, 1)
    one.core_done()
    one.step(1)
    outer(1, 2)
    two.core_send(0, 0, 4)
    grad_halo.take_rest(0)
    two.core_done()
    two.step(1)
    grad_halo.take_rest(1)

    gacc[...] = jnp.zeros_like(gacc)
    stores = []

    def backward(f, half):
        left = jnp.concatenate(
            [
                gout[f + 2 - t // 3, 2 * half + 2 - t % 3 : 2 * half + 4 - t % 3].reshape(2 * WD, CH)
                for t in range(9)
            ],
            axis=1,
        )
        right = jnp.concatenate([wgt[3 * t : 3 * t + 3].reshape(3 * CH, CH) for t in range(9)], axis=1)
        prod[f, 0 : 2 * WD] = lax.dot_general(left, right, (((1,), (1,)), ((), ())), preferred_element_type=F32)

        def one_row(i, _):
            r = 2 * half + i
            at = pl.ds(pl.multiple_of(i * WD, WD), WD)
            grad_soft = up(prod[f, at, 0:CH]) + prod[f, at, CH : 2 * CH] + down(prod[f, at, 2 * CH : 3 * CH])
            _, inverse, normed = normalise(lat[f, r])
            grad_act = grad_soft * slope(normed * g_row)
            per_cell = grad_act * normed
            gacc[...] += jnp.sum(per_cell.reshape(WD // 8, 8, CH), axis=0)
            scaled = grad_act * g_row
            mean = jnp.mean(per_cell * g_row, axis=-1, keepdims=True)
            res[f, r] = (gout[f, 1 + r].astype(F32) + inverse * (scaled - normed * mean)).astype(BF)
            return 0

        lax.fori_loop(0, 2, one_row, 0)
        pair = pl.ds(2 * half, 2)
        store = pltpu.make_async_copy(res.at[f, pair], out_lat.at[f, pair], osem.at[2 * f + half])
        store.start()
        stores.append(store)

    backward(0, 0)
    one.step(2)
    backward(0, 1)
    two.step(2)
    backward(1, 0)
    one.step(3)
    backward(1, 1)

    gt[tm] = gacc[...]
    gain_copies = [
        send(gacc, gt.at[tm], gss.at[d - 1], grs.at[d - 1], {"tm": (tm + d) % 8, "rows": row}) for d in range(1, 8)
    ]

    two.step(3)

    for copy in gain_copies:
        copy.wait()
    gsum = gt[0]
    for d in range(1, 8):
        gsum = gsum + gt[d]
    gmid[0] = gsum
    gx[place[1]] = gsum
    xcopies = [
        send(gmid.at[0], gx.at[place[1]], gss.at[6 + q], grs.at[6 + q], peer(1, q)) for q in (1, 2, 3)
    ]

    one.step(4)

    for copy in xcopies:
        copy.wait()
    gsum = gx[0] + gx[1] + gx[2] + gx[3]
    gmid[1] = gsum
    gz[place[2]] = gsum
    zcopies = [
        send(gmid.at[1], gz.at[place[2]], gss.at[9 + q], grs.at[9 + q], peer(2, q)) for q in (1, 2, 3)
    ]

    two.step(4)
    for copy in zcopies:
        copy.wait()
    gsum = gz[0] + gz[1] + gz[2] + gz[3]
    out_gain[...] = jnp.sum(gsum, axis=0)
    for store in stores:
        store.wait()
    soft_halo.finish()
    grad_halo.finish()
    one.last()
    one.finish()
    two.last()
    two.finish()


def hand_on(*refs):
    sems = refs[6]
    copies = [pltpu.make_async_copy(refs[i], refs[3 + i], sems.at[i]) for i in range(3)]
    for copy in copies:
        copy.start()
    for copy in copies:
        copy.wait()


def shards(latents, reward_weight, norm_gain, conv_weight, scored_frames):
    vm = pl.BlockSpec(memory_space=pltpu.VMEM)
    anywhere = pl.BlockSpec(memory_space=pl.ANY)
    dma = pltpu.SemaphoreType.DMA
    units = lambda n: pltpu.VMEM((n * SUB, 128), BF)
    shapes = (
        jax.ShapeDtypeStruct((FR, HT, WD, CH), BF),
        jax.ShapeDtypeStruct((OWN, CH), F32),
        jax.ShapeDtypeStruct((CH,), F32),
    )
    results = pl.pallas_call(
        kernel,
        out_shape=shapes,
        in_specs=[anywhere, anywhere, vm, anywhere, pl.BlockSpec(memory_space=pltpu.SMEM)],
        out_specs=(anywhere, vm, vm),
        scratch_shapes=[
            pltpu.VMEM((FR, HT, WD, CH), BF),
            pltpu.VMEM((FR, HT, WD, CH), BF),
            pltpu.VMEM((FR, HT, WD, CH), BF),
            pltpu.VMEM((27, CH, CH), BF),
            pltpu.VMEM((4, HT + 2, WD, CH), BF),
            pltpu.VMEM((CH, 4 * (HT + 2) * WD), BF),
            pltpu.VMEM((4, HT + 2, WD, CH), BF),
            pltpu.VMEM((FR * FLAT, 3 * CH), BF),
            pltpu.VMEM((FR, FLAT, 3 * CH), F32),
            pltpu.VMEM((3, TAPROWS + 16, 128), F32),
            units(576),
            pltpu.VMEM((12 * SLAB, 128), BF),
            units(288),
            units(144),
            units(108),
            units(27),
            pltpu.VMEM((3, PAD, 128), F32),
            pltpu.VMEM((8, CH), F32),
            pltpu.VMEM((8, 8, CH), F32),
            pltpu.VMEM((4, 8, CH), F32),
            pltpu.VMEM((4, 8, CH), F32),
            pltpu.VMEM((2, 8, CH), F32),
            dma((3,)),
            dma((4,)),
            dma((14,)),
            dma((14,)),
            dma((14,)),
            dma((14,)),
            dma((6,)),
            dma((6,)),
            dma((48,)),
            dma((48,)),
            dma((13,)),
            dma((13,)),
        ],
        compiler_params=pltpu.CompilerParams(
            collective_id=0, has_side_effects=True, vmem_limit_bytes=61 * 1024 * 1024
        ),
        cost_estimate=pl.CostEstimate(flops=24_500_000_000, bytes_accessed=12_000_000, transcendentals=1_500_000),
    )(latents, reward_weight, norm_gain, conv_weight, scored_frames)
    return tuple(
        pl.pallas_call(
            hand_on,
            out_shape=shapes,
            in_specs=[vm] * 3,
            out_specs=(anywhere,) * 3,
            scratch_shapes=[dma((3,))],
        )(*results)
    )


def solution(mesh):
    placed = (P("tm", "rows", None, None), P("tm", "rows", None, None), P(), P(), P())
    return jax.shard_map(
        shards,
        mesh=mesh,
        in_specs=placed,
        out_specs=(P("tm", "rows", None, None), P(("tm", "rows"), None), P()),
        check_vma=False,
    )
```

```python
import functools

import jax
import jax.numpy as jnp
from jax import lax
from jax.experimental import pallas as pl
from jax.experimental.pallas import tpu as pltpu
from jax.sharding import PartitionSpec as P

MESH = pl.DeviceIdType.MESH
EPSILON = 1e-06
BF = jnp.bfloat16
F32 = jnp.float32
FR, HT, WD, CH = 2, 4, 128, 384
FLAT = HT * WD
OWN = 81
PAD = 96
SUB = 32
SLAB = 16 * OWN
TAPROWS = 27 * CH
ORDERS = ((0, 1, 2), (1, 2, 0), (2, 0, 1))
CHUNKS = ((0, 1), (2,))


def sigmoid(value):
    return 0.5 + 0.5 * jnp.tanh(0.5 * value)


def slope(value):
    s = sigmoid(value)
    return s * (1.0 + value * (1.0 - s))


def normalise(cells):
    wide = cells.astype(F32)
    inverse = lax.rsqrt(jnp.mean(wide * wide, axis=-1, keepdims=True) + EPSILON)
    return wide, inverse, wide * inverse


def down(x):
    row = lax.broadcasted_iota(jnp.int32, x.shape, 0)
    return jnp.where(row == 0, 0.0, pltpu.roll(x, 1, 0))


def up(x):
    row = lax.broadcasted_iota(jnp.int32, x.shape, 0)
    return jnp.where(row == x.shape[0] - 1, 0.0, pltpu.roll(x, x.shape[0] - 1, 0))


def kernel(
    lat_hbm, rew_hbm, gain, wgt_hbm, scored,
    out_lat, out_w, out_gain,
    lat, rew, res, wgt, ext, extt, gout, gsh, prod, gw,
    cs, cr, r1, r2, r3, r4, fin,
    gacc, gt, gx, gz, gmid,
    wsem, osem, hs, hr, ks, kr, css, crs, ss, rs, gss, grs,
):
    tm = lax.axis_index("tm")
    row = lax.axis_index("rows")
    core = tm % 2
    place = (tm // 2, row // 4, row % 4)

    def device(coords, c):
        return {"tm": coords[0] * 2 + c, "rows": coords[1] * 4 + coords[2]}

    def flip(v):
        return v + 1 - 2 * (v % 2)

    other = []
    for v in place:
        second = core * flip(v) + (1 - core) * (3 - v)
        first = core * (3 - v) + (1 - core) * flip(v)
        other.append((v, second, first, (v + 2) % 4))

    def peer(axis, q):
        coords = list(place)
        coords[axis] = other[axis][q]
        return device(coords, core)

    def pick(axis, q):
        if isinstance(q, int):
            return other[axis][q]
        o = other[axis]
        return jnp.where(q == 0, o[0], jnp.where(q == 1, o[1], jnp.where(q == 2, o[2], o[3])))

    row_next, row_prev = (row + 1) % 16, (row + 15) % 16
    twin = {"tm": tm + 1 - 2 * core, "rows": row}

    barrier = pltpu.get_barrier_semaphore()
    partners = [{"tm": tm, "rows": row_next}, {"tm": tm, "rows": row_prev}]
    partners += [{"tm": (tm + d) % 8, "rows": row} for d in range(1, 8)]
    partners += [peer(axis, q) for axis in (1, 2) for q in (1, 2, 3)]
    for partner in partners:
        pl.semaphore_signal(barrier, 1, device_id=partner, device_id_type=MESH)

    load_lat = pltpu.make_async_copy(lat_hbm, lat, wsem.at[0])
    load = pltpu.make_async_copy(wgt_hbm, wgt, wsem.at[1])
    load_rew = pltpu.make_async_copy(rew_hbm, rew, wsem.at[2])
    load_lat.start()
    load.start()
    load_rew.start()

    g_row = gain[...].reshape(1, CH)
    zero_block = jnp.zeros((2, WD, CH), BF)

    def own_soft(i, _):
        f, r = i // HT, i % HT
        _, _, normed = normalise(lat[f, r])
        act = normed * g_row
        ext[2 + f, 1 + r] = (act * sigmoid(act)).astype(BF)
        return 0

    load_lat.wait()
    lax.fori_loop(0, FR * HT, own_soft, 0)

    def product(f, taps):
        left = jnp.concatenate(
            [ext[f + a, b : b + HT].reshape(FLAT, CH) for a, b in taps], axis=1
        )
        right = jnp.concatenate(
            [jnp.concatenate([wgt[9 * a + 3 * b + c] for c in range(3)], axis=1) for a, b in taps], axis=0
        )
        return jnp.dot(left, right, preferred_element_type=F32)

    load.wait()
    prod[0] = product(0, [(2, 1)])
    prod[1] = product(1, [(1, 1), (2, 1)])

    pl.semaphore_wait(barrier, len(partners))

    def copy_of(src, dst, a, b, target):
        return pltpu.make_async_remote_copy(
            src_ref=src, dst_ref=dst, send_sem=a, recv_sem=b, device_id=target, device_id_type=MESH
        )

    def send(*args):
        copy = copy_of(*args)
        copy.start()
        return copy

    class Halo:
        def __init__(self, ref, own, far, step, order, sems):
            self.own, self.far, self.ref, self.order = own, far, ref, order
            self.giver = core == (0 if step == 1 else 1)
            self.end = 0 if step == 1 else 7
            up_row, down_row = {"tm": tm, "rows": row_next}, {"tm": tm, "rows": row_prev}
            slab = {"tm": (tm + step) % 8, "rows": row}
            mine = pl.ds(own, 2)
            theirs = pl.ds(far, 2)

            def make(i, src, dst, target):
                return copy_of(src, dst, sems[0].at[i], sems[1].at[i], target)

            self.rows = [
                make(0, ref.at[mine, HT], ref.at[mine, 0], up_row),
                make(1, ref.at[mine, 1], ref.at[mine, HT + 1], down_row),
            ]
            self.edges, self.inner, self.relay = {}, {}, {}
            for k in order:
                self.edges[k] = [
                    make(2 + 2 * k, ref.at[own + k, HT], ref.at[far + k, HT], slab),
                    make(3 + 2 * k, ref.at[own + k, 1], ref.at[far + k, 1], slab),
                ]
                inside = pl.ds(2, HT - 2)
                self.inner[k] = [make(6 + k, ref.at[own + k, inside], ref.at[far + k, inside], slab)]
                self.relay[k] = [
                    make(10 + 2 * k, ref.at[far + k, HT], ref.at[far + k, 0], up_row),
                    make(11 + 2 * k, ref.at[far + k, 1], ref.at[far + k, HT + 1], down_row),
                ]
            self.forward = [
                make(8, ref.at[mine, 0], ref.at[theirs, 0], twin),
                make(9, ref.at[mine, HT + 1], ref.at[theirs, HT + 1], twin),
            ]

        def begin(self):
            for copy in self.rows:
                copy.start()
            for k in self.order:
                for copy in self.edges[k]:
                    copy.start()
            for k in self.order:
                for copy in self.inner[k]:
                    copy.start()

        def take_rows(self):
            for copy in self.rows:
                copy.wait_recv()
            self.clear(self.own, 2)

            @pl.when(self.giver)
            def _():
                for copy in self.forward:
                    copy.start()

        def take_edges(self, k):
            for copy in self.edges[k]:
                copy.wait_recv()

            @pl.when(self.giver)
            def _():
                for copy in self.relay[k]:
                    copy.start()

        def take_rest(self, k):
            for copy in self.inner[k]:
                copy.wait_recv()

            @pl.when(self.giver)
            def _():
                for copy in self.relay[k]:
                    copy.wait()

            if k == self.order[0]:

                @pl.when(jnp.logical_not(self.giver))
                def _():
                    for copy in self.forward:
                        copy.wait_recv()

            self.clear(self.far + k, 1)

            @pl.when(tm == self.end)
            def _():
                self.ref[self.far + k] = jnp.zeros((HT + 2, WD, CH), BF)

        def clear(self, frame, count):
            @pl.when(row == 0)
            def _():
                self.ref[frame : frame + count, 0] = zero_block[:count]

            @pl.when(row == 15)
            def _():
                self.ref[frame : frame + count, HT + 1] = zero_block[:count]

        def finish(self):
            @pl.when(self.giver)
            def _():
                for copy in self.forward:
                    copy.wait_send()

            for copy in self.rows:
                copy.wait_send()
            for k in self.order:
                for copy in self.edges[k] + self.inner[k]:
                    copy.wait_send()

    soft_halo = Halo(ext, 2, 0, 1, (1, 0), (hs, hr))
    soft_halo.begin()

    def turn(f, rows):
        for r in rows:
            extt[:, (f * 6 + r) * WD : (f * 6 + r + 1) * WD] = ext[f, r].T

    def emit(f):
        frame = tm * FR + f
        mask = jnp.float32(0.0)
        for i in range(8):
            mask = jnp.maximum(mask, jnp.where(scored[i] == frame, 1.0, 0.0))

        def one_row(r, _):
            at = pl.ds(pl.multiple_of(r * WD, WD), WD)
            conv = down(prod[f, at, 0:CH]) + prod[f, at, CH : 2 * CH] + up(prod[f, at, 2 * CH : 3 * CH])
            value = lat[f, r].astype(F32) + conv
            grad = mask * rew[f, r].astype(F32) * slope(value)
            low = grad.astype(BF)
            wide = low.astype(F32)
            gout[f, 1 + r] = low
            to = pl.ds(pl.multiple_of(f * FLAT + r * WD, WD), WD)
            for c, shifted in enumerate((up(wide).astype(BF), low, down(wide).astype(BF))):
                gsh[to, c * 256 : c * 256 + 256] = shifted[:, :256]
                gsh[to, 768 + c * 128 : 896 + c * 128] = shifted[:, 256:]
            return 0

        lax.fori_loop(0, HT, one_row, 0)

    for f in (2, 3):
        turn(f, (1, 2, 3, 4))
    soft_halo.take_rows()
    prod[0] += product(0, [(2, 0), (2, 2)])
    soft_halo.take_edges(1)
    prod[1] += product(1, [(1, 0), (1, 2), (2, 0), (2, 2)])
    load_rew.wait()
    for f in (2, 3):
        turn(f, (0, 5))
    soft_halo.take_edges(0)
    soft_halo.take_rest(1)
    prod[1] += product(1, [(0, 0), (0, 1), (0, 2)])
    emit(1)
    prod[0] += product(0, [(1, 0), (1, 1), (1, 2)])
    turn(1, range(6))
    soft_halo.take_rest(0)
    prod[0] += product(0, [(0, 0), (0, 1), (0, 2)])
    emit(0)

    grad_halo = Halo(gout, 0, 2, -1, (0, 1), (ks, kr))
    grad_halo.begin()

    turn(0, range(6))
    gw[:, TAPROWS:, :] = jnp.zeros((3, 16, 128), F32)

    def start_of(block):
        return ((block * OWN) >> 4) << 4

    def unit(n, count=1):
        return pl.ds(pl.multiple_of(SUB * n, SUB), SUB * count)

    class Chunk:
        def __init__(self, n):
            self.parts = CHUNKS[n]
            self.width = len(self.parts)
            self.base = 3 * sum(len(c) for c in CHUNKS[:n])
            self.sem = 24 * n
            self.csem = 3 * n
            self.core_copies = []
            self.copies = {}

        def area(self, blocks):
            return self.base * blocks

        def core_send(self, n, low, high):
            lead = self.base * 64 * SUB
            for k in range(low, high):
                for pi, p in enumerate(self.parts):
                    at = lead + (k * self.width + pi) * SLAB

                    def one(i, _):
                        step = SLAB // 9
                        src = pl.multiple_of((2 * k + 1 - core) * SLAB + i * step, 16)
                        dst = pl.multiple_of(at + i * step, 16)
                        cs[pl.ds(dst, step)] = gw[p, pl.ds(src, step)].astype(BF)
                        return 0

                    lax.fori_loop(0, 9, one, 0)
            rows = self.width * (high - low) * SLAB
            src = pl.ds(lead + low * self.width * SLAB, rows)
            dst = pl.ds(self.base // 3 * 4 * SLAB + low * self.width * SLAB, rows)
            self.core_copies.append(
                send(cs.at[src], cr.at[dst], css.at[self.csem + n], crs.at[self.csem + n], twin)
            )

        def core_done(self):
            for copy in self.core_copies:
                copy.wait()

        def rows_of(self, j, q):
            coords = [None, None, None]
            for axis, at in zip(ORDERS[j], q):
                coords[axis] = pick(axis, at)
            slab = 2 * coords[0] + core
            start = start_of(slab * 16 + coords[1] * 4 + coords[2]) + SUB * j
            return start, (self.base // 3 * 4 + coords[0] * self.width - slab) * SLAB + start

        def total(self, pi, rows):
            held = gw[self.parts[pi], pl.ds(pl.multiple_of(rows[0], 16), SUB)]
            return held + cr[pl.ds(pl.multiple_of(rows[1] + pi * SLAB, 16), SUB)].astype(F32)

        def got(self, ref, blocks, j, i, pi):
            return ref[unit(self.area(blocks) + (j * blocks + i) * self.width + pi)].astype(F32)

        def value(self, step, pi, j, q, rows):
            value = self.total(pi, rows)
            if step >= 2:
                value = value + self.got(r1, 32, j, (q[0] * 4 + q[1]) * 4 + q[2], pi)
            if step >= 3:
                value = value + self.got(r2, 16, j, q[1] * 4 + q[2], pi)
            if step >= 4:
                for n in range(3):
                    value = value + self.got(r3, 12, j, 4 * n + q[2], pi)
            if step >= 5:
                for n in range(3):
                    value = value + self.got(r4, 3, j, n, pi)
            return value

        def step(self, step):
            if step > 1:
                for copy in self.copies[step - 1]:
                    copy.wait_recv()
            first = (None, 0, 96, 144, 180)[step]
            blocks = (None, 32, 16, 12, 3)[step]
            into = (None, r1, r2, r3, r4)[step]
            lead = self.area(64) + first * self.width

            firsts = (None, (2, 3), (1,), (0,), (0,))[step]
            thirds = (1, 2, 3) if step == 4 else (0, 1, 2, 3)
            low, high = ((0, 0), (0, 4), (0, 4), (1, 4), (0, 1))[step]

            def one(q2, _):
                for q1 in firsts:
                    for q3 in thirds:
                        i = q3 - 1 if step == 4 else (q1 - firsts[0]) * 16 + (q2 - low) * 4 + q3
                        for j in range(3):
                            q = (q1, q2, q3)
                            rows = self.rows_of(j, q)
                            for pi in range(self.width):
                                value = self.value(step, pi, j, q, rows).astype(BF)
                                cs[unit(lead + (j * blocks + i) * self.width + pi)] = value
                return 0

            if step == 4:
                one(0, 0)
            else:
                lax.fori_loop(low, high, one, 0)
            out = []
            for j in range(3):
                axis = ORDERS[j][(None, 0, 0, 1, 2)[step]]
                for n, q in enumerate(((2,), (1,), (1, 2, 3), (1, 2, 3))[step - 1]):
                    span = blocks // (1 if step < 3 else 3) * self.width
                    at = j * blocks * self.width + n * span
                    sem = self.sem + (None, j, 3 + j, 6 + 3 * j + n, 15 + 3 * j + n)[step]
                    out.append(
                        send(
                            cs.at[unit(lead + at, span)],
                            into.at[unit(self.area(blocks) + at, span)],
                            ss.at[sem],
                            rs.at[sem],
                            peer(axis, q),
                        )
                    )
            self.copies[step] = out

        def last(self):
            for copy in self.copies[4]:
                copy.wait_recv()
            for pi, p in enumerate(self.parts):
                for j in range(3):
                    fin[p, SUB * j : SUB * j + SUB] = self.value(5, pi, j, (0, 0, 0), self.rows_of(j, (0, 0, 0)))
            offset = (tm * 16 + row) * OWN % 16
            for p in self.parts:
                out_w[:, p * 128 : p * 128 + 128] = fin[p, pl.ds(offset, OWN)]

        def finish(self):
            for copies in self.copies.values():
                for copy in copies:
                    copy.wait_send()

    def outer(n, a):
        parts = CHUNKS[n]
        wide = 128 * len(parts)
        left = jnp.concatenate(
            [
                jnp.concatenate(
                    [extt[:, ((f + a) * 6 + b) * WD : ((f + a) * 6 + b) * WD + FLAT] for f in range(FR)], axis=1
                )
                for b in range(3)
            ],
            axis=0,
        )
        lanes = slice(384 * parts[0], 384 * parts[0] + 3 * wide)
        part = jnp.dot(left, gsh[:, lanes], preferred_element_type=F32)
        for b in range(3):
            for c in range(3):
                at = (9 * a + 3 * b + c) * CH
                for pi, p in enumerate(parts):
                    lane = c * wide + pi * 128
                    gw[p, at : at + CH, :] = part[b * CH : b * CH + CH, lane : lane + 128]

    one, two = Chunk(0), Chunk(1)
    outer(0, 0)
    one.core_send(0, 0, 1)
    outer(0, 1)
    one.core_send(1, 1, 2)
    grad_halo.take_rows()
    outer(0, 2)
    one.core_send(2, 2, 4)
    grad_halo.take_edges(0)
    outer(1, 0)
    grad_halo.take_edges(1)
    outer(1, 1)
    one.core_done()
    one.step(1)
    outer(1, 2)
    two.core_send(0, 0, 4)
    grad_halo.take_rest(0)
    two.core_done()
    two.step(1)
    grad_halo.take_rest(1)

    gacc[...] = jnp.zeros_like(gacc)
    stores = []

    def backward(f, half):
        left = jnp.concatenate(
            [
                gout[f + 2 - t // 3, 2 * half + 2 - t % 3 : 2 * half + 4 - t % 3].reshape(2 * WD, CH)
                for t in range(9)
            ],
            axis=1,
        )
        right = jnp.concatenate([wgt[3 * t : 3 * t + 3].reshape(3 * CH, CH) for t in range(9)], axis=1)
        prod[f, 0 : 2 * WD] = lax.dot_general(left, right, (((1,), (1,)), ((), ())), preferred_element_type=F32)

        def one_row(i, _):
            r = 2 * half + i
            at = pl.ds(pl.multiple_of(i * WD, WD), WD)
            grad_soft = up(prod[f, at, 0:CH]) + prod[f, at, CH : 2 * CH] + down(prod[f, at, 2 * CH : 3 * CH])
            _, inverse, normed = normalise(lat[f, r])
            grad_act = grad_soft * slope(normed * g_row)
            per_cell = grad_act * normed
            gacc[...] += jnp.sum(per_cell.reshape(WD // 8, 8, CH), axis=0)
            scaled = grad_act * g_row
            mean = jnp.mean(per_cell * g_row, axis=-1, keepdims=True)
            res[f, r] = (gout[f, 1 + r].astype(F32) + inverse * (scaled - normed * mean)).astype(BF)
            return 0

        lax.fori_loop(0, 2, one_row, 0)
        pair = pl.ds(2 * half, 2)
        store = pltpu.make_async_copy(res.at[f, pair], out_lat.at[f, pair], osem.at[2 * f + half])
        store.start()
        stores.append(store)

    backward(0, 0)
    one.step(2)
    backward(0, 1)
    two.step(2)
    backward(1, 0)
    one.step(3)
    backward(1, 1)

    gt[tm] = gacc[...]
    gain_copies = [
        send(gacc, gt.at[tm], gss.at[d - 1], grs.at[d - 1], {"tm": (tm + d) % 8, "rows": row}) for d in range(1, 8)
    ]

    two.step(3)

    for copy in gain_copies:
        copy.wait()
    gsum = gt[0]
    for d in range(1, 8):
        gsum = gsum + gt[d]
    gmid[0] = gsum
    gx[place[1]] = gsum
    xcopies = [
        send(gmid.at[0], gx.at[place[1]], gss.at[6 + q], grs.at[6 + q], peer(1, q)) for q in (1, 2, 3)
    ]

    one.step(4)

    for copy in xcopies:
        copy.wait()
    gsum = gx[0] + gx[1] + gx[2] + gx[3]
    gmid[1] = gsum
    gz[place[2]] = gsum
    zcopies = [
        send(gmid.at[1], gz.at[place[2]], gss.at[9 + q], grs.at[9 + q], peer(2, q)) for q in (1, 2, 3)
    ]

    two.step(4)
    for copy in zcopies:
        copy.wait()
    gsum = gz[0] + gz[1] + gz[2] + gz[3]
    out_gain[...] = jnp.sum(gsum, axis=0)
    for store in stores:
        store.wait()
    soft_halo.finish()
    grad_halo.finish()
    one.last()
    one.finish()
    two.last()
    two.finish()


def hand_on(*refs):
    sems = refs[6]
    copies = [pltpu.make_async_copy(refs[i], refs[3 + i], sems.at[i]) for i in range(3)]
    for copy in copies:
        copy.start()
    for copy in copies:
        copy.wait()


def shards(latents, reward_weight, norm_gain, conv_weight, scored_frames):
    vm = pl.BlockSpec(memory_space=pltpu.VMEM)
    anywhere = pl.BlockSpec(memory_space=pl.ANY)
    dma = pltpu.SemaphoreType.DMA
    units = lambda n: pltpu.VMEM((n * SUB, 128), BF)
    shapes = (
        jax.ShapeDtypeStruct((FR, HT, WD, CH), BF),
        jax.ShapeDtypeStruct((OWN, CH), F32),
        jax.ShapeDtypeStruct((CH,), F32),
    )
    results = pl.pallas_call(
        kernel,
        out_shape=shapes,
        in_specs=[anywhere, anywhere, vm, anywhere, pl.BlockSpec(memory_space=pltpu.SMEM)],
        out_specs=(anywhere, vm, vm),
        scratch_shapes=[
            pltpu.VMEM((FR, HT, WD, CH), BF),
            pltpu.VMEM((FR, HT, WD, CH), BF),
            pltpu.VMEM((FR, HT, WD, CH), BF),
            pltpu.VMEM((27, CH, CH), BF),
            pltpu.VMEM((4, HT + 2, WD, CH), BF),
            pltpu.VMEM((CH, 4 * (HT + 2) * WD), BF),
            pltpu.VMEM((4, HT + 2, WD, CH), BF),
            pltpu.VMEM((FR * FLAT, 3 * CH), BF),
            pltpu.VMEM((FR, FLAT, 3 * CH), F32),
            pltpu.VMEM((3, TAPROWS + 16, 128), F32),
            units(576),
            pltpu.VMEM((12 * SLAB, 128), BF),
            units(288),
            units(144),
            units(108),
            units(27),
            pltpu.VMEM((3, PAD, 128), F32),
            pltpu.VMEM((8, CH), F32),
            pltpu.VMEM((8, 8, CH), F32),
            pltpu.VMEM((4, 8, CH), F32),
            pltpu.VMEM((4, 8, CH), F32),
            pltpu.VMEM((2, 8, CH), F32),
            dma((3,)),
            dma((4,)),
            dma((14,)),
            dma((14,)),
            dma((14,)),
            dma((14,)),
            dma((6,)),
            dma((6,)),
            dma((48,)),
            dma((48,)),
            dma((13,)),
            dma((13,)),
        ],
        compiler_params=pltpu.CompilerParams(
            collective_id=0, has_side_effects=True, vmem_limit_bytes=61 * 1024 * 1024
        ),
        cost_estimate=pl.CostEstimate(flops=24_500_000_000, bytes_accessed=12_000_000, transcendentals=1_500_000),
    )(latents, reward_weight, norm_gain, conv_weight, scored_frames)
    return tuple(
        pl.pallas_call(
            hand_on,
            out_shape=shapes,
            in_specs=[vm] * 3,
            out_specs=(anywhere,) * 3,
            scratch_shapes=[dma((3,))],
        )(*results)
    )


def solution(mesh):
    placed = (P("tm", "rows", None, None), P("tm", "rows", None, None), P(), P(), P())
    return jax.shard_map(
        shards,
        mesh=mesh,
        in_specs=placed,
        out_specs=(P("tm", "rows", None, None), P(("tm", "rows"), None), P()),
        check_vma=False,
    )
```
